32 devices in a mesh: chain: 4 (over z), param: 8 (over y, x, core).
Axes of the slice: x: 2, y: 2, z: 4, core: 2. Of those that a mesh axis runs over, the one named last changes fastest.
Arguments:
- spins: int32 [128, 256, 4], P(('chain', 'param')), may hold values from 0 to 1
- local_energy: float32 [128], replicated, may hold values from -24 to 24
- embed_weight: float32 [4, 256], replicated, may hold values from -3 to 3
- position: bfloat16 [256, 256], replicated, may hold values from -6 to 6
- value_weight: bfloat16 [256, 256], replicated, may hold values from -0.375 to 0.375
- mixing: bfloat16 [8, 256, 256], replicated, may hold values from -0.375 to 0.375
- out_weight: bfloat16 [256, 256], replicated, may hold values from -0.375 to 0.375
- up_weight: bfloat16 [256, 1024], replicated, may hold values from -0.375 to 0.375
- down_weight: bfloat16 [1024, 256], replicated, may hold values from -0.1875 to 0.1875
- readout: float32 [256], replicated, may hold values from -6 to 6
Outputs:
- up_update: float32 [256, 1024], P('chain', 'param')
- down_update: float32 [1024, 256], P('param', 'chain')
- sample_weights: float32 [128], replicated
The draws below stay inside these ranges and needn't reach their ends.
All inputs are finite; a program needn't handle non-finite values.
Results may differ from the reference program's by a relative error of at most 0.018.
Values may be sent and summed in bfloat16 or wider, within the bound.
A program may use at most 128 MiB of HBM per device.

```python
import math
import jax
import jax.numpy as jnp
from jax import lax

D = 256
HEADS = 8
FF = 1024
PATCHES = 256
NS = 128
N_PARAM = 8


def with_ends(result, stream_key, low, top_value):
    longest = result.shape.index(max(result.shape))
    spots = []
    for shift in (0, 1):
        where = [jax.random.randint(jax.random.fold_in(stream_key, axis), (), 0, length) for axis, length in enumerate(result.shape)]
        where[longest] = (where[longest] + shift) % result.shape[longest]
        spots.append(tuple(where))
    return result.at[spots[0]].set(low).at[spots[1]].set(top_value)


def noise(key, extent, scale, limit, kind=jnp.bfloat16):
    result = jax.random.normal(key, extent, jnp.float32) * scale
    return jnp.minimum(jnp.maximum(result, -limit), limit).astype(kind)


def setup_inputs(seed: int = 0) -> dict:
    key_of = jax.random.split(jax.random.key(seed), 11)
    return {
        "spins": with_ends(jax.random.randint(key_of[0], (NS, PATCHES, 4), 0, 2), jax.random.fold_in(key_of[0], 1), 0, 1).astype(jnp.int32),
        "local_energy": noise(key_of[1], (NS,), 4.0, 24.0, jnp.float32),
        "embed_weight": noise(key_of[2], (4, D), 4 ** -0.5, 3.0, jnp.float32),
        "position": noise(key_of[3], (PATCHES, D), 1.0, 6.0),
        "value_weight": noise(key_of[4], (D, D), D ** -0.5, 0.375),
        "mixing": noise(key_of[5], (HEADS, PATCHES, PATCHES), PATCHES ** -0.5, 0.375),
        "out_weight": noise(key_of[6], (D, D), D ** -0.5, 0.375),
        "up_weight": noise(key_of[7], (D, FF), D ** -0.5, 0.375),
        "down_weight": noise(key_of[8], (FF, D), FF ** -0.5, 0.1875),
        "readout": noise(key_of[9], (D,), 1.0, 6.0, jnp.float32),
    }


damping = 0.05

def layer_norm(hidden_state):
    average = lax.optimization_barrier(jnp.mean(hidden_state, axis=-1, keepdims=True))
    centred = hidden_state - average
    spread = lax.optimization_barrier(jnp.mean(centred * centred, axis=-1, keepdims=True))
    return centred * lax.rsqrt(spread + 1e-05)

def project(operand, weights):
    return lax.dot_general(operand.astype(jnp.float32), weights.astype(jnp.float32), (((operand.ndim - 1,), (0,)), ((), ())), preferred_element_type=jnp.float32)

def solve_weights(gram, local_energy, total):
    scale = jnp.trace(gram) / total
    system = gram + damping * scale * jnp.eye(total, dtype=jnp.float32)
    lower = jnp.linalg.cholesky(system)
    energy = (local_energy - jnp.mean(local_energy)) / math.sqrt(total)
    column = energy[:, None]
    middle = lax.linalg.triangular_solve(lower, column, left_side=True, lower=True)
    answer = lax.linalg.triangular_solve(lower, middle, left_side=True, lower=True, transpose_a=True)
    return scale * answer[:, 0]

def reference(spins, local_energy, embed_weight, position, value_weight, mixing, out_weight, up_weight, down_weight, readout):
    total = spins.shape[0]
    head_count = mixing.shape[0]
    model_width = value_weight.shape[0]
    spin_values = (2 * spins - 1).astype(jnp.float32)
    embedded = lax.optimization_barrier(jnp.sum(spin_values[..., None] * embed_weight, axis=2)) + position.astype(jnp.float32)
    normed = layer_norm(embedded).astype(jnp.bfloat16)
    values = project(normed, value_weight).astype(jnp.bfloat16)
    split_values = values.reshape(total, PATCHES, head_count, model_width // head_count)
    mixture = jnp.einsum('htu,suhe->sthe', mixing.astype(jnp.float32), split_values.astype(jnp.float32))
    mixture = mixture.astype(jnp.bfloat16).reshape(total, PATCHES, model_width)
    residual = embedded + project(mixture, out_weight)
    features = layer_norm(residual).astype(jnp.bfloat16)
    preact = project(features, up_weight)
    hidden = jax.nn.gelu(preact).astype(jnp.bfloat16)
    output = residual + project(hidden, down_weight)
    cotangent = (readout * jnp.tanh(output)).astype(jnp.bfloat16)
    backward = lax.dot_general(cotangent.astype(jnp.float32), down_weight.astype(jnp.float32), (((2,), (1,)), ((), ())), preferred_element_type=jnp.float32)
    preact_grad = jax.vjp(jax.nn.gelu, preact)[1](backward)[0].astype(jnp.bfloat16)
    block = FF // N_PARAM
    features_wide = features.astype(jnp.float32)
    cotangent_wide = cotangent.astype(jnp.float32)

    def jac_block(block_index):
        offset = (block_index * block).astype(jnp.int32)
        grad_part = lax.dynamic_slice_in_dim(preact_grad, offset, block, 2).astype(jnp.float32)
        hidden_part = lax.dynamic_slice_in_dim(hidden, offset, block, 2).astype(jnp.float32)
        up_block = jnp.einsum('sti,stj->sij', features_wide, grad_part)
        down_block = jnp.einsum('std,stj->sdj', cotangent_wide, hidden_part)
        jac = jnp.stack([up_block, down_block], axis=1).astype(jnp.bfloat16).reshape(total, -1)
        jac_wide = jac.astype(jnp.float32)
        return (jac_wide - lax.optimization_barrier(jnp.mean(jac_wide, axis=0))) / math.sqrt(total)
    indices = jnp.arange(N_PARAM, dtype=jnp.int32)

    def add_gram(carry, block_index):
        centred = jac_block(block_index)
        term = lax.dot_general(centred.astype(jnp.float32), centred.astype(jnp.float32), (((1,), (1,)), ((), ())), precision=lax.Precision.HIGHEST, preferred_element_type=jnp.float32)
        return (carry + term, None)
    gram, _unused = lax.scan(add_gram, jnp.zeros((total, total), jnp.float32), indices)
    sample_weights = solve_weights(gram, local_energy, total)

    def update_block(block_index):
        centred = jac_block(block_index)
        moved = lax.dot_general(sample_weights.astype(jnp.float32), centred.astype(jnp.float32), (((0,), (0,)), ((), ())), precision=lax.Precision.HIGHEST, preferred_element_type=jnp.float32)
        return -moved.reshape(2, model_width, block)
    blocks = lax.map(update_block, indices)
    up_update = jnp.transpose(blocks[:, 0], (1, 0, 2)).reshape(model_width, N_PARAM * block)
    down_update = jnp.transpose(blocks[:, 1], (0, 2, 1)).reshape(N_PARAM * block, model_width)
    return (up_update, down_update, sample_weights)
```

```python
import functools
import math

import jax
import jax.numpy as jnp
from jax import lax
from jax.experimental import pallas as pl
from jax.experimental.pallas import tpu as pltpu
from jax.sharding import PartitionSpec as P

damping = 0.05
MESH = pl.DeviceIdType.MESH
slope = math.sqrt(2.0 / math.pi)
cubic = 0.044715


def dot(a, b, dims=((1,), (0,))):
    return lax.dot_general(a, b, (dims, ((), ())), preferred_element_type=jnp.float32)


def norm_columns(v):
    width = v.shape[0]
    centred = v - jnp.sum(v, axis=0, keepdims=True) * (1.0 / width)
    spread = jnp.sum(centred * centred, axis=0, keepdims=True) * (1.0 / width)
    return (centred * lax.rsqrt(spread + 1e-05)).astype(jnp.bfloat16)


def greet(count, peer_of):
    barrier = pltpu.get_barrier_semaphore()

    def tell(k, carry):
        pl.semaphore_signal(barrier, inc=1, device_id=peer_of(k), device_id_type=MESH)
        return carry

    lax.fori_loop(1, count, tell, 0)
    pl.semaphore_wait(barrier, count - 1)


def gather_kernel(chips, per_plane, mine, out, send_sem, recv_sem):
    z, p = lax.axis_index("chain"), lax.axis_index("param")
    me = z * per_plane + p // 2

    def peer_of(k):
        q = lax.rem(me + k, chips)
        return (q // per_plane, 2 * lax.rem(q, per_plane) + lax.rem(p, 2))

    greet(chips, peer_of)

    def copy_to(k):
        return pltpu.make_async_remote_copy(
            src_ref=mine,
            dst_ref=out.at[me],
            send_sem=send_sem.at[k],
            recv_sem=recv_sem.at[k],
            device_id=peer_of(k),
            device_id_type=MESH,
        )

    def start(k, carry):
        copy_to(k).start()
        return carry

    def wait(k, carry):
        copy_to(k).wait()
        return carry

    lax.fori_loop(1, chips, start, 0)
    out[me] = mine[...]
    lax.fori_loop(1, chips, wait, 0)


def sum_kernel(count, per_row, parts, out, landed, total, sems):
    z, p = lax.axis_index("chain"), lax.axis_index("param")
    me = z * per_row + p

    def peer_of(k):
        q = lax.rem(me + k, count)
        return (q // per_row, lax.rem(q, per_row))

    greet(count, peer_of)

    def scatter(k):
        return pltpu.make_async_remote_copy(
            src_ref=parts.at[lax.rem(me + k, count)],
            dst_ref=landed.at[me],
            send_sem=sems.at[0, k],
            recv_sem=sems.at[1, k],
            device_id=peer_of(k),
            device_id_type=MESH,
        )

    def spread(k):
        return pltpu.make_async_remote_copy(
            src_ref=total,
            dst_ref=out.at[me],
            send_sem=sems.at[2, k],
            recv_sem=sems.at[3, k],
            device_id=peer_of(k),
            device_id_type=MESH,
        )

    def run(make, verb):
        def step(k, carry):
            getattr(make(k), verb)()
            return carry

        lax.fori_loop(1, count, step, 0)

    run(scatter, "start")
    landed[me] = parts[me]
    run(scatter, "wait")
    total[...] = jnp.sum(landed[...], axis=0)
    run(spread, "start")
    out[me] = total[...]
    run(spread, "wait")


def forward_kernel(
    depth, spins, embed, position, value_t, mixing, out_t, up_t, down_t, down_own, readout, jac, wide
):
    z = lax.axis_index("chain")
    core = lax.rem(lax.axis_index("param"), 2)
    group, heads = embed.shape[0], mixing.shape[0]
    width = value_t.shape[0]
    head_rows = width // heads
    both = down_own.shape[0]
    shard = both // 2
    chunk = min(256, up_t.shape[0])
    chunks = up_t.shape[0] // chunk
    base = position[...].astype(jnp.float32)
    triple = jnp.concatenate([spins[0]] * 3, axis=0)
    embedded = [dot(embed[k], triple) + base for k in range(group)]
    values = [dot(value_t[...], norm_columns(e)).astype(jnp.bfloat16) for e in embedded]
    mixed = []
    for h in range(heads):
        rows = slice(h * head_rows, (h + 1) * head_rows)
        stacked = jnp.concatenate([v[rows] for v in values], axis=0)
        mixed.append(dot(stacked, mixing[h], ((1,), (1,))).astype(jnp.bfloat16))
    slab = pl.ds(pl.multiple_of(z * depth, depth), depth)
    for k in range(group):
        rows = slice(k * head_rows, (k + 1) * head_rows)
        mixture = jnp.concatenate([m[rows] for m in mixed], axis=0)
        residual = embedded[k] + dot(out_t[...], mixture)
        features = norm_columns(residual)
        output = residual
        for c in range(chunks):
            rows = slice(c * chunk, (c + 1) * chunk)
            preact = dot(up_t[rows], features)
            squared = preact * preact
            bend = jnp.tanh(preact * (slope + (slope * cubic) * squared))
            half = 0.5 + 0.5 * bend
            hidden = (preact * half).astype(jnp.bfloat16)
            if c == 0:
                own_hidden = hidden[:both]
                x, s, b = preact[:both], squared[:both], bend[:both]
                rise = half[:both] + (0.5 * x) * (1.0 - b * b) * (slope + (3.0 * slope * cubic) * s)
            output = output + dot(down_t[:, rows], hidden)
        cotangent = (readout[...] * jnp.tanh(output)).astype(jnp.bfloat16)
        grad = (rise * dot(down_own[...], cotangent)).astype(jnp.bfloat16)
        wide[k % 2, 0] = features
        wide[k % 2, 1] = cotangent
        up_block = dot(wide[k % 2, 0, slab, :], grad, ((1,), (1,))).astype(jnp.bfloat16)
        down_block = dot(wide[k % 2, 1, slab, :], own_hidden, ((1,), (1,))).astype(jnp.bfloat16)
        for side in range(2):
            columns = slice(side * shard, (side + 1) * shard)
            where = jnp.bitwise_xor(core, side)
            jac[where, 0, k, :depth, :] = up_block[:, columns]
            jac[where, 0, k, depth:, :] = down_block[:, columns]


def solve_weights(gram, energy, total):
    scale = jnp.trace(gram) / total
    system = gram + damping * scale * jnp.eye(total, dtype=jnp.float32)
    lower = jnp.linalg.cholesky(system)
    column = energy[:, None]
    middle = lax.linalg.triangular_solve(lower, column, left_side=True, lower=True)
    answer = lax.linalg.triangular_solve(
        lower, middle, left_side=True, lower=True, transpose_a=True
    )
    return scale * answer[:, 0]


def body(
    n_chain,
    n_param,
    spins,
    local_energy,
    embed_weight,
    position,
    value_weight,
    mixing,
    out_weight,
    up_weight,
    down_weight,
    readout,
):
    samples, patches, sites = spins.shape
    total = local_energy.shape[0]
    width, hidden_units = up_weight.shape
    heads = mixing.shape[0]
    count = n_chain * n_param
    chips, per_plane = count // 2, n_param // 2
    depth, shard = width // n_chain, hidden_units // n_param
    both = 2 * shard
    vmem = pl.BlockSpec(memory_space=pltpu.VMEM)
    core = lax.axis_index("param") % 2
    offset = (lax.axis_index("param") // 2) * both

    signs = (2 * spins - 1).astype(jnp.bfloat16)
    signs = signs.transpose(0, 2, 1).reshape(samples * sites, patches)
    all_signs = pl.pallas_call(
        functools.partial(gather_kernel, chips, per_plane),
        out_shape=jax.ShapeDtypeStruct((chips, samples * sites, patches), jnp.bfloat16),
        in_specs=[vmem],
        out_specs=vmem,
        scratch_shapes=[pltpu.SemaphoreType.DMA((chips,)), pltpu.SemaphoreType.DMA((chips,))],
        compiler_params=pltpu.CompilerParams(collective_id=0, has_side_effects=True),
    )(signs)

    high = lax.reduce_precision(embed_weight, 8, 7)
    middle = lax.reduce_precision(embed_weight - high, 8, 7)
    low = embed_weight - high - middle
    parts = jnp.stack([high, middle, low]).astype(jnp.bfloat16)
    pick = jnp.eye(samples, dtype=jnp.bfloat16)
    embed = jnp.einsum("kg,acd->kdagc", pick, parts).reshape(samples, width, 3 * samples * sites)

    def turned(weights):
        return lax.dynamic_slice_in_dim(
            jnp.concatenate([weights, weights], axis=0), offset, hidden_units, 0
        )

    down_turned = turned(down_weight)
    whole = lambda *shape: pl.BlockSpec(shape, lambda g: (0,) * len(shape))
    jac = pl.pallas_call(
        functools.partial(forward_kernel, depth),
        grid=(chips,),
        out_shape=jax.ShapeDtypeStruct((2, chips, samples, 2 * depth, shard), jnp.bfloat16),
        in_specs=[
            pl.BlockSpec((1, samples * sites, patches), lambda g: (g, 0, 0)),
            whole(*embed.shape),
            whole(width, patches),
            whole(width, width),
            whole(*mixing.shape),
            whole(width, width),
            whole(hidden_units, width),
            whole(width, hidden_units),
            whole(both, width),
            whole(width, 1),
        ],
        out_specs=pl.BlockSpec((2, 1, samples, 2 * depth, shard), lambda g: (0, g, 0, 0, 0)),
        scratch_shapes=[pltpu.VMEM((2, 2, width, patches), jnp.bfloat16)],
        compiler_params=pltpu.CompilerParams(vmem_limit_bytes=48 * 2**20),
    )(
        all_signs,
        embed,
        position.T,
        value_weight.T,
        mixing,
        out_weight.T,
        turned(up_weight.T),
        down_turned.T,
        down_turned[:both],
        readout[:, None],
    )
    sibling = lax.ppermute(jac[1], "param", [(i, i ^ 1) for i in range(n_param)])
    rows = jnp.stack([jac[0], sibling]).reshape(total, 2 * depth * shard)
    raw = lax.dot_general(
        rows, rows, (((1,), (1,)), ((), ())), preferred_element_type=jnp.float32
    ).reshape(2, total // 2, 2, total // 2)
    raw = jnp.where(core == 1, raw[::-1, :, ::-1], raw)
    raw = pl.pallas_call(
        functools.partial(sum_kernel, count, n_param),
        out_shape=jax.ShapeDtypeStruct((count, samples, total), jnp.float32),
        in_specs=[vmem],
        out_specs=vmem,
        scratch_shapes=[
            pltpu.VMEM((count, samples, total), jnp.float32),
            pltpu.VMEM((samples, total), jnp.float32),
            pltpu.SemaphoreType.DMA((4, count)),
        ],
        compiler_params=pltpu.CompilerParams(collective_id=1, has_side_effects=True),
    )(raw.reshape(count, samples, total)).reshape(total, total)
    average = jnp.mean(raw, axis=0)
    gram = (raw - average[None, :] - average[:, None] + jnp.mean(average)) / total
    energy = (local_energy - jnp.mean(local_energy)) / math.sqrt(total)
    energy = energy.reshape(chips, 2, samples).swapaxes(0, 1).reshape(total)
    solved = solve_weights(gram, energy, total)
    sample_weights = solved.reshape(2, chips, samples).swapaxes(0, 1).reshape(total)
    pull = ((solved - jnp.mean(solved)) * (-1.0 / math.sqrt(total))).reshape(2, total // 2)
    pull = jnp.where(core == 1, pull[::-1], pull).reshape(total)
    update = jnp.sum(pull[:, None] * rows.astype(jnp.float32), axis=0).reshape(2, depth, shard)
    return (update[0], update[1].T, sample_weights)


def solution(mesh):
    in_specs = (P(("chain", "param"), None, None), P(), P(), P(), P(), P(), P(), P(), P(), P())
    out_specs = (P("chain", "param"), P("param", "chain"), P())
    run = functools.partial(body, mesh.shape["chain"], mesh.shape["param"])
    return jax.shard_map(run, mesh=mesh, in_specs=in_specs, out_specs=out_specs, check_vma=False)
```

```python
import functools
import math

import jax
import jax.numpy as jnp
from jax import lax
from jax.experimental import pallas as pl
from jax.experimental.pallas import tpu as pltpu
from jax.sharding import PartitionSpec as P

damping = 0.05
MESH = pl.DeviceIdType.MESH
slope = math.sqrt(2.0 / math.pi)
cubic = 0.044715


def dot(a, b, dims=((1,), (0,))):
    return lax.dot_general(a, b, (dims, ((), ())), preferred_element_type=jnp.float32)


def norm_columns(v):
    width = v.shape[0]
    centred = v - jnp.sum(v, axis=0, keepdims=True) * (1.0 / width)
    spread = jnp.sum(centred * centred, axis=0, keepdims=True) * (1.0 / width)
    return (centred * lax.rsqrt(spread + 1e-05)).astype(jnp.bfloat16)


def greet(count, peer_of):
    barrier = pltpu.get_barrier_semaphore()

    def tell(k, carry):
        pl.semaphore_signal(barrier, inc=1, device_id=peer_of(k), device_id_type=MESH)
        return carry

    lax.fori_loop(1, count, tell, 0)
    pl.semaphore_wait(barrier, count - 1)


def sum_kernel(count, per_row, parts, out, landed, total, sems):
    z, p = lax.axis_index("chain"), lax.axis_index("param")
    me = z * per_row + p

    def peer_of(k):
        q = lax.rem(me + k, count)
        return (q // per_row, lax.rem(q, per_row))

    greet(count, peer_of)

    def scatter(k):
        return pltpu.make_async_remote_copy(
            src_ref=parts.at[lax.rem(me + k, count)],
            dst_ref=landed.at[me],
            send_sem=sems.at[0, k],
            recv_sem=sems.at[1, k],
            device_id=peer_of(k),
            device_id_type=MESH,
        )

    def spread(k):
        return pltpu.make_async_remote_copy(
            src_ref=total,
            dst_ref=out.at[me],
            send_sem=sems.at[2, k],
            recv_sem=sems.at[3, k],
            device_id=peer_of(k),
            device_id_type=MESH,
        )

    def run(make, verb):
        def step(k, carry):
            getattr(make(k), verb)()
            return carry

        lax.fori_loop(1, count, step, 0)

    run(scatter, "start")
    landed[me] = parts[me]
    run(scatter, "wait")
    total[...] = jnp.sum(landed[...], axis=0)
    run(spread, "start")
    out[me] = total[...]
    run(spread, "wait")


def forward_kernel(
    n_chain,
    n_param,
    mine,
    embed,
    position,
    value_t,
    mixing,
    out_t,
    up_t,
    down_t,
    down,
    readout,
    jac,
    spins,
    stage,
    wide,
    spin_sems,
    send_sem,
    recv_sem,
):
    z, p = lax.axis_index("chain"), lax.axis_index("param")
    group, heads = embed.shape[0], mixing.shape[0]
    width, hidden_units = down_t.shape
    head_rows, depth, shard = width // heads, width // n_chain, hidden_units // n_param
    chunk = min(256, hidden_units)
    chunks = hidden_units // chunk

    barrier = pltpu.get_barrier_semaphore()

    def tell_chain(k, carry):
        there = (lax.rem(z + n_chain - k, n_chain), p)
        pl.semaphore_signal(barrier, inc=1, device_id=there, device_id_type=MESH)
        return carry

    def tell_plane(m, carry):
        there = (z, lax.rem(p + m, n_param))
        pl.semaphore_signal(barrier, inc=1, device_id=there, device_id_type=MESH)
        return carry

    lax.fori_loop(1, n_chain, tell_chain, 0)
    lax.fori_loop(1, n_param, tell_plane, 0)
    pl.semaphore_wait(barrier, n_chain + n_param - 2)

    def spin_copy(k):
        return pltpu.make_async_remote_copy(
            src_ref=mine,
            dst_ref=spins.at[z],
            send_sem=spin_sems.at[0, k],
            recv_sem=spin_sems.at[1, k],
            device_id=(lax.rem(z + n_chain - k, n_chain), p),
            device_id_type=MESH,
        )

    def slice_copy(g, k, m):
        owner = lax.rem(p + m, n_param)
        return pltpu.make_async_remote_copy(
            src_ref=stage.at[g, k, owner],
            dst_ref=jac.at[p, g, k],
            send_sem=send_sem.at[g, k, m],
            recv_sem=recv_sem.at[g, k, m],
            device_id=(z, owner),
            device_id_type=MESH,
        )

    def start_spins(k, carry):
        spin_copy(k).start()
        return carry

    lax.fori_loop(1, n_chain, start_spins, 0)
    spins[z] = mine[...]
    slab = pl.ds(pl.multiple_of(z * depth, depth), depth)

    def one_group(step, carry):
        @pl.when(step > 0)
        def _():
            spin_copy(step).wait_recv()

        g = lax.rem(z + step, n_chain)
        base = position[...].astype(jnp.float32)
        triple = jnp.concatenate([spins[g]] * 3, axis=0)
        embedded = [dot(embed[k], triple) + base for k in range(group)]
        values = [dot(value_t[...], norm_columns(e)).astype(jnp.bfloat16) for e in embedded]
        mixed = []
        for h in range(heads):
            rows = slice(h * head_rows, (h + 1) * head_rows)
            stacked = jnp.concatenate([v[rows] for v in values], axis=0)
            mixed.append(dot(stacked, mixing[h], ((1,), (1,))).astype(jnp.bfloat16))
        for k in range(group):
            rows = slice(k * head_rows, (k + 1) * head_rows)
            mixture = jnp.concatenate([m[rows] for m in mixed], axis=0)
            residual = embedded[k] + dot(out_t[...], mixture)
            features = norm_columns(residual)
            output = residual
            units, rises = [], []
            for c in range(chunks):
                rows = slice(c * chunk, (c + 1) * chunk)
                preact = dot(up_t[rows], features)
                squared = preact * preact
                bend = jnp.tanh(preact * (slope + (slope * cubic) * squared))
                half = 0.5 + 0.5 * bend
                hidden = (preact * half).astype(jnp.bfloat16)
                units.append(hidden)
                rises.append(
                    half
                    + (0.5 * preact)
                    * (1.0 - bend * bend)
                    * (slope + (3.0 * slope * cubic) * squared)
                )
                output = output + dot(down_t[:, rows], hidden)
            cotangent = (readout[...] * jnp.tanh(output)).astype(jnp.bfloat16)
            wide[k % 2, 0] = features
            wide[k % 2, 1] = cotangent
            left, right = wide[k % 2, 0, slab, :], wide[k % 2, 1, slab, :]
            for c in range(chunks):
                rows = slice(c * chunk, (c + 1) * chunk)
                grad = (rises[c] * dot(down[rows], cotangent)).astype(jnp.bfloat16)
                up_block = dot(left, grad, ((1,), (1,))).astype(jnp.bfloat16)
                down_block = dot(right, units[c], ((1,), (1,))).astype(jnp.bfloat16)
                for part in range(chunk // shard):
                    columns = slice(part * shard, (part + 1) * shard)
                    owner = c * (chunk // shard) + part
                    stage[g, k, owner, :depth, :] = up_block[:, columns]
                    stage[g, k, owner, depth:, :] = down_block[:, columns]

            def start_slices(m, carry):
                slice_copy(g, k, m).start()
                return carry

            lax.fori_loop(1, n_param, start_slices, 0)
            jac[p, g, k] = stage[g, k, p]
        return carry

    lax.fori_loop(0, n_chain, one_group, 0)

    def end_spins(k, carry):
        spin_copy(k).wait_send()
        return carry

    lax.fori_loop(1, n_chain, end_spins, 0)

    def end_slices(i, carry):
        m = 1 + lax.rem(i, n_param - 1)
        gk = i // (n_param - 1)
        slice_copy(gk // group, lax.rem(gk, group), m).wait()
        return carry

    lax.fori_loop(0, n_chain * group * (n_param - 1), end_slices, 0)


def solve_weights(gram, energy, total):
    scale = jnp.trace(gram) / total
    system = gram + damping * scale * jnp.eye(total, dtype=jnp.float32)
    lower = jnp.linalg.cholesky(system)
    column = energy[:, None]
    middle = lax.linalg.triangular_solve(lower, column, left_side=True, lower=True)
    answer = lax.linalg.triangular_solve(
        lower, middle, left_side=True, lower=True, transpose_a=True
    )
    return scale * answer[:, 0]


def body(
    n_chain,
    n_param,
    spins,
    local_energy,
    embed_weight,
    position,
    value_weight,
    mixing,
    out_weight,
    up_weight,
    down_weight,
    readout,
):
    samples, patches, sites = spins.shape
    total = local_energy.shape[0]
    width, hidden_units = up_weight.shape
    heads = mixing.shape[0]
    count = n_chain * n_param
    depth, shard = width // n_chain, hidden_units // n_param
    vmem = pl.BlockSpec(memory_space=pltpu.VMEM)

    signs = (2 * spins - 1).astype(jnp.bfloat16)
    signs = signs.transpose(0, 2, 1).reshape(samples * sites, patches)
    high = lax.reduce_precision(embed_weight, 8, 7)
    middle = lax.reduce_precision(embed_weight - high, 8, 7)
    low = embed_weight - high - middle
    parts = jnp.stack([high, middle, low]).astype(jnp.bfloat16)
    pick = jnp.eye(samples, dtype=jnp.bfloat16)
    embed = jnp.einsum("kg,acd->kdagc", pick, parts).reshape(samples, width, 3 * samples * sites)

    sems = (n_chain, samples, n_param)
    jac = pl.pallas_call(
        functools.partial(forward_kernel, n_chain, n_param),
        out_shape=jax.ShapeDtypeStruct(
            (n_param, n_chain, samples, 2 * depth, shard), jnp.bfloat16
        ),
        in_specs=[vmem] * 10,
        out_specs=vmem,
        scratch_shapes=[
            pltpu.VMEM((n_chain, samples * sites, patches), jnp.bfloat16),
            pltpu.VMEM((n_chain, samples, n_param, 2 * depth, shard), jnp.bfloat16),
            pltpu.VMEM((2, 2, width, patches), jnp.bfloat16),
            pltpu.SemaphoreType.DMA((2, n_chain)),
            pltpu.SemaphoreType.DMA(sems),
            pltpu.SemaphoreType.DMA(sems),
        ],
        compiler_params=pltpu.CompilerParams(
            collective_id=0, has_side_effects=True, vmem_limit_bytes=56 * 2**20
        ),
    )(
        signs,
        embed,
        position.T,
        value_weight.T,
        mixing,
        out_weight.T,
        up_weight.T,
        down_weight.T,
        down_weight,
        readout[:, None],
    )
    rows = jac.reshape(total, 2 * depth * shard)
    raw = lax.dot_general(
        rows, rows, (((1,), (1,)), ((), ())), preferred_element_type=jnp.float32
    )
    raw = pl.pallas_call(
        functools.partial(sum_kernel, count, n_param),
        out_shape=jax.ShapeDtypeStruct((count, samples, total), jnp.float32),
        in_specs=[vmem],
        out_specs=vmem,
        scratch_shapes=[
            pltpu.VMEM((count, samples, total), jnp.float32),
            pltpu.VMEM((samples, total), jnp.float32),
            pltpu.SemaphoreType.DMA((4, count)),
        ],
        compiler_params=pltpu.CompilerParams(collective_id=1, has_side_effects=True),
    )(raw.reshape(count, samples, total)).reshape(total, total)
    average = jnp.mean(raw, axis=0)
    gram = (raw - average[None, :] - average[:, None] + jnp.mean(average)) / total
    energy = (local_energy - jnp.mean(local_energy)) / math.sqrt(total)
    energy = energy.reshape(n_chain, n_param, samples).swapaxes(0, 1).reshape(total)
    solved = solve_weights(gram, energy, total)
    sample_weights = solved.reshape(n_param, n_chain, samples).swapaxes(0, 1).reshape(total)
    pull = (solved - jnp.mean(solved)) * (-1.0 / math.sqrt(total))
    update = jnp.sum(pull[:, None] * rows.astype(jnp.float32), axis=0).reshape(2, depth, shard)
    return (update[0], update[1].T, sample_weights)


def solution(mesh):
    in_specs = (P(("chain", "param"), None, None), P(), P(), P(), P(), P(), P(), P(), P(), P())
    out_specs = (P("chain", "param"), P("param", "chain"), P())
    run = functools.partial(body, mesh.shape["chain"], mesh.shape["param"])
    return jax.shard_map(run, mesh=mesh, in_specs=in_specs, out_specs=out_specs, check_vma=False)
```

```python
import functools
import math

import jax
import jax.numpy as jnp
from jax import lax
from jax.experimental import pallas as pl
from jax.experimental.pallas import tpu as pltpu
from jax.sharding import PartitionSpec as P

damping = 0.05
MESH = pl.DeviceIdType.MESH
slope = math.sqrt(2.0 / math.pi)
cubic = 0.044715


def dot(a, b, dims=((1,), (0,))):
    return lax.dot_general(a, b, (dims, ((), ())), preferred_element_type=jnp.float32)


def norm_columns(v):
    width = v.shape[0]
    centred = v - jnp.sum(v, axis=0, keepdims=True) * (1.0 / width)
    spread = jnp.sum(centred * centred, axis=0, keepdims=True) * (1.0 / width)
    return (centred * lax.rsqrt(spread + 1e-05)).astype(jnp.bfloat16)


def greet(count, peer_of):
    barrier = pltpu.get_barrier_semaphore()

    def tell(k, carry):
        pl.semaphore_signal(barrier, inc=1, device_id=peer_of(k), device_id_type=MESH)
        return carry

    lax.fori_loop(1, count, tell, 0)
    pl.semaphore_wait(barrier, count - 1)


def sum_kernel(count, per_row, parts, out, landed, total, sems):
    z, p = lax.axis_index("chain"), lax.axis_index("param")
    me = z * per_row + p

    def peer_of(k):
        q = lax.rem(me + k, count)
        return (q // per_row, lax.rem(q, per_row))

    greet(count, peer_of)

    def scatter(k):
        return pltpu.make_async_remote_copy(
            src_ref=parts.at[lax.rem(me + k, count)],
            dst_ref=landed.at[me],
            send_sem=sems.at[0, k],
            recv_sem=sems.at[1, k],
            device_id=peer_of(k),
            device_id_type=MESH,
        )

    def spread(k):
        return pltpu.make_async_remote_copy(
            src_ref=total,
            dst_ref=out.at[me],
            send_sem=sems.at[2, k],
            recv_sem=sems.at[3, k],
            device_id=peer_of(k),
            device_id_type=MESH,
        )

    def run(make, verb):
        def step(k, carry):
            getattr(make(k), verb)()
            return carry

        lax.fori_loop(1, count, step, 0)

    run(scatter, "start")
    landed[me] = parts[me]
    run(scatter, "wait")
    total[...] = jnp.sum(landed[...], axis=0)
    run(spread, "start")
    out[me] = total[...]
    run(spread, "wait")


def forward_kernel(
    n_chain,
    n_param,
    mine,
    embed,
    position,
    value,
    mixing,
    out,
    up,
    down,
    readout,
    jac,
    position_t,
    value_t,
    out_t,
    up_t,
    down_t,
    readout_t,
    spins,
    stage,
    wide,
    spin_sems,
    send_sem,
    recv_sem,
):
    z, p = lax.axis_index("chain"), lax.axis_index("param")
    group, heads = embed.shape[0], mixing.shape[0]
    width, hidden_units = down_t.shape
    head_rows, depth, shard = width // heads, width // n_chain, hidden_units // n_param
    chunk = min(256, hidden_units)
    chunks = hidden_units // chunk

    barrier = pltpu.get_barrier_semaphore()

    def tell_chain(k, carry):
        there = (lax.rem(z + n_chain - k, n_chain), p)
        pl.semaphore_signal(barrier, inc=1, device_id=there, device_id_type=MESH)
        return carry

    def tell_plane(m, carry):
        there = (z, lax.rem(p + m, n_param))
        pl.semaphore_signal(barrier, inc=1, device_id=there, device_id_type=MESH)
        return carry

    lax.fori_loop(1, n_chain, tell_chain, 0)
    lax.fori_loop(1, n_param, tell_plane, 0)
    pl.semaphore_wait(barrier, n_chain + n_param - 2)

    def spin_copy(k):
        return pltpu.make_async_remote_copy(
            src_ref=mine,
            dst_ref=spins.at[z],
            send_sem=spin_sems.at[0, k],
            recv_sem=spin_sems.at[1, k],
            device_id=(lax.rem(z + n_chain - k, n_chain), p),
            device_id_type=MESH,
        )

    def slice_copy(g, k, m):
        owner = lax.rem(p + m, n_param)
        return pltpu.make_async_remote_copy(
            src_ref=stage.at[g, k, owner],
            dst_ref=jac.at[p, g, k],
            send_sem=send_sem.at[g, k, m],
            recv_sem=recv_sem.at[g, k, m],
            device_id=(z, owner),
            device_id_type=MESH,
        )

    def start_spins(k, carry):
        spin_copy(k).start()
        return carry

    lax.fori_loop(1, n_chain, start_spins, 0)
    spins[z] = mine[...]
    position_t[...] = position[...].astype(jnp.float32).T
    value_t[...] = value[...].T
    out_t[...] = out[...].T
    up_t[...] = up[...].T
    down_t[...] = down[...].T
    readout_t[...] = jnp.broadcast_to(readout[...], readout_t.shape[::-1]).T
    slab = pl.ds(pl.multiple_of(z * depth, depth), depth)

    def one_group(step, carry):
        @pl.when(step > 0)
        def _():
            spin_copy(step).wait_recv()

        g = lax.rem(z + step, n_chain)
        base = position_t[...]
        triple = jnp.concatenate([spins[g]] * 3, axis=0)
        embedded = [dot(embed[k], triple, ((0,), (0,))) + base for k in range(group)]
        values = [dot(value_t[...], norm_columns(e)).astype(jnp.bfloat16) for e in embedded]
        mixed = []
        for h in range(heads):
            rows = slice(h * head_rows, (h + 1) * head_rows)
            stacked = jnp.concatenate([v[rows] for v in values], axis=0)
            mixed.append(dot(stacked, mixing[h], ((1,), (1,))).astype(jnp.bfloat16))
        for k in range(group):
            rows = slice(k * head_rows, (k + 1) * head_rows)
            mixture = jnp.concatenate([m[rows] for m in mixed], axis=0)
            residual = embedded[k] + dot(out_t[...], mixture)
            features = norm_columns(residual)
            output = residual
            units, rises = [], []
            for c in range(chunks):
                rows = slice(c * chunk, (c + 1) * chunk)
                preact = dot(up_t[rows], features)
                squared = preact * preact
                bend = jnp.tanh(preact * (slope + (slope * cubic) * squared))
                half = 0.5 + 0.5 * bend
                hidden = (preact * half).astype(jnp.bfloat16)
                units.append(hidden)
                rises.append(
                    half
                    + (0.5 * preact)
                    * (1.0 - bend * bend)
                    * (slope + (3.0 * slope * cubic) * squared)
                )
                output = output + dot(down_t[:, rows], hidden)
            cotangent = (readout_t[...] * jnp.tanh(output)).astype(jnp.bfloat16)
            wide[k % 2, 0] = features
            wide[k % 2, 1] = cotangent
            left, right = wide[k % 2, 0, slab, :], wide[k % 2, 1, slab, :]
            for c in range(chunks):
                rows = slice(c * chunk, (c + 1) * chunk)
                grad = (rises[c] * dot(down[rows], cotangent)).astype(jnp.bfloat16)
                up_block = dot(left, grad, ((1,), (1,))).astype(jnp.bfloat16)
                down_block = dot(right, units[c], ((1,), (1,))).astype(jnp.bfloat16)
                for part in range(chunk // shard):
                    columns = slice(part * shard, (part + 1) * shard)
                    owner = c * (chunk // shard) + part
                    stage[g, k, owner, :depth, :] = up_block[:, columns]
                    stage[g, k, owner, depth:, :] = down_block[:, columns]

            def start_slices(m, carry):
                slice_copy(g, k, m).start()
                return carry

            lax.fori_loop(1, n_param, start_slices, 0)
            jac[p, g, k] = stage[g, k, p]
        return carry

    lax.fori_loop(0, n_chain, one_group, 0)

    def end_spins(k, carry):
        spin_copy(k).wait_send()
        return carry

    lax.fori_loop(1, n_chain, end_spins, 0)

    def end_slices(i, carry):
        m = 1 + lax.rem(i, n_param - 1)
        gk = i // (n_param - 1)
        slice_copy(gk // group, lax.rem(gk, group), m).wait()
        return carry

    lax.fori_loop(0, n_chain * group * (n_param - 1), end_slices, 0)


def solve_kernel(raw, energy, solved):
    size = raw.shape[0]
    tile = 8
    gram = raw[...]
    by_row = jnp.mean(gram, axis=0, keepdims=True)
    by_column = jnp.mean(gram, axis=1, keepdims=True)
    gram = (gram - by_row - by_column + jnp.mean(by_row, axis=1, keepdims=True)) * (1.0 / size)
    row = lax.broadcasted_iota(jnp.int32, (size, size), 0)
    column = lax.broadcasted_iota(jnp.int32, (size, size), 1)
    same = row == column
    diagonal = jnp.sum(jnp.where(same, gram, 0.0), axis=0, keepdims=True)
    scale = jnp.sum(diagonal, axis=1, keepdims=True) * (1.0 / size)
    system = gram + jnp.where(same, damping * scale, 0.0)
    right = jnp.broadcast_to(energy[...], (size, size)).T
    rest = jnp.concatenate([system, right], axis=1)
    sub = lax.broadcasted_iota(jnp.int32, (tile, size), 0)
    lane = lax.broadcasted_iota(jnp.int32, (tile, size), 1)

    def across(block, i):
        return jnp.broadcast_to(block[i : i + 1], block.shape)

    saved = []
    for start in range(0, size, tile):
        left, aim = rest[:tile, :size], rest[:tile, size:]
        columns = [
            jnp.broadcast_to(left[:, start + j : start + j + 1], (tile, size)) for j in range(tile)
        ]
        inverse = jnp.zeros((tile, size), jnp.float32)
        for i in range(tile):
            over = 1.0 / across(columns[i], i)
            inverse = jnp.where(sub == i, over, inverse)
            factor = jnp.where(sub > i, columns[i] * over, 0.0)
            left = left - factor * across(left, i)
            aim = aim - factor * across(aim, i)
            for j in range(i + 1, tile):
                columns[j] = columns[j] - factor * across(columns[j], i)
        saved.append((left, aim, columns, inverse))
        if start + tile < size:
            scaled = jnp.concatenate([left * inverse, aim * inverse], axis=1)
            taken = lax.dot_general(
                left,
                scaled,
                (((0,), (0,)), ((), ())),
                precision=lax.Precision.HIGHEST,
                preferred_element_type=jnp.float32,
            )
            rest = rest[tile:] - taken[start + tile :]
    answer = jnp.zeros((tile, size), jnp.float32)
    for start in range(size - tile, -1, -tile):
        left, aim, columns, inverse = saved[start // tile]
        aim = aim - jnp.sum(left * answer, axis=1, keepdims=True)
        for i in range(tile - 1, -1, -1):
            found = across(aim * inverse, i)
            answer = jnp.where(lane == start + i, found, answer)
            aim = aim - columns[i] * found
    solved[...] = answer[:1] * scale


def solve_weights(gram, energy, total):
    scale = jnp.trace(gram) / total
    system = gram + damping * scale * jnp.eye(total, dtype=jnp.float32)
    lower = jnp.linalg.cholesky(system)
    column = energy[:, None]
    middle = lax.linalg.triangular_solve(lower, column, left_side=True, lower=True)
    answer = lax.linalg.triangular_solve(
        lower, middle, left_side=True, lower=True, transpose_a=True
    )
    return scale * answer[:, 0]


def body(
    n_chain,
    n_param,
    spins,
    local_energy,
    embed_weight,
    position,
    value_weight,
    mixing,
    out_weight,
    up_weight,
    down_weight,
    readout,
):
    samples, patches, sites = spins.shape
    total = local_energy.shape[0]
    width, hidden_units = up_weight.shape
    heads = mixing.shape[0]
    count = n_chain * n_param
    depth, shard = width // n_chain, hidden_units // n_param
    vmem = pl.BlockSpec(memory_space=pltpu.VMEM)

    signs = (2 * spins - 1).astype(jnp.bfloat16)
    signs = signs.transpose(0, 2, 1).reshape(samples * sites, patches)
    high = lax.reduce_precision(embed_weight, 8, 7)
    middle = lax.reduce_precision(embed_weight - high, 8, 7)
    low = embed_weight - high - middle
    parts = jnp.stack([high, middle, low]).astype(jnp.bfloat16)
    pick = jnp.eye(samples, dtype=jnp.bfloat16)
    embed = pick[:, None, :, None, None] * parts[:, None, :, :]
    embed = embed.reshape(samples, 3 * samples * sites, width)

    sems = (n_chain, samples, n_param)
    jac = pl.pallas_call(
        functools.partial(forward_kernel, n_chain, n_param),
        out_shape=jax.ShapeDtypeStruct(
            (n_param, n_chain, samples, 2 * depth, shard), jnp.bfloat16
        ),
        in_specs=[vmem] * 9,
        out_specs=vmem,
        scratch_shapes=[
            pltpu.VMEM((width, patches), jnp.float32),
            pltpu.VMEM((width, width), jnp.bfloat16),
            pltpu.VMEM((width, width), jnp.bfloat16),
            pltpu.VMEM((hidden_units, width), jnp.bfloat16),
            pltpu.VMEM((width, hidden_units), jnp.bfloat16),
            pltpu.VMEM((width, patches), jnp.float32),
            pltpu.VMEM((n_chain, samples * sites, patches), jnp.bfloat16),
            pltpu.VMEM((n_chain, samples, n_param, 2 * depth, shard), jnp.bfloat16),
            pltpu.VMEM((2, 2, width, patches), jnp.bfloat16),
            pltpu.SemaphoreType.DMA((2, n_chain)),
            pltpu.SemaphoreType.DMA(sems),
            pltpu.SemaphoreType.DMA(sems),
        ],
        compiler_params=pltpu.CompilerParams(
            collective_id=0, has_side_effects=True, vmem_limit_bytes=56 * 2**20
        ),
    )(
        signs,
        embed,
        position,
        value_weight,
        mixing,
        out_weight,
        up_weight,
        down_weight,
        readout[None, :],
    )
    rows = lax.optimization_barrier(jac.reshape(total, 2 * depth * shard))
    raw = lax.dot_general(
        rows, rows, (((1,), (1,)), ((), ())), preferred_element_type=jnp.float32
    )
    raw = pl.pallas_call(
        functools.partial(sum_kernel, count, n_param),
        out_shape=jax.ShapeDtypeStruct((count, samples, total), jnp.float32),
        in_specs=[vmem],
        out_specs=vmem,
        scratch_shapes=[
            pltpu.VMEM((count, samples, total), jnp.float32),
            pltpu.VMEM((samples, total), jnp.float32),
            pltpu.SemaphoreType.DMA((4, count)),
        ],
        compiler_params=pltpu.CompilerParams(collective_id=1, has_side_effects=True),
    )(raw.reshape(count, samples, total)).reshape(total, total)
    energy = (local_energy - jnp.mean(local_energy)) / math.sqrt(total)
    energy = energy.reshape(n_chain, n_param, samples).swapaxes(0, 1).reshape(total)
    if total <= 128 and total % 8 == 0:
        solved = pl.pallas_call(
            solve_kernel,
            out_shape=jax.ShapeDtypeStruct((1, total), jnp.float32),
            in_specs=[vmem, vmem],
            out_specs=vmem,
            compiler_params=pltpu.CompilerParams(vmem_limit_bytes=24 * 2**20),
        )(raw, energy[None, :])[0]
    else:
        average = jnp.mean(raw, axis=0)
        gram = (raw - average[None, :] - average[:, None] + jnp.mean(average)) / total
        solved = solve_weights(gram, energy, total)
    sample_weights = solved.reshape(n_param, n_chain, samples).swapaxes(0, 1).reshape(total)
    pull = (solved - jnp.mean(solved)) * (-1.0 / math.sqrt(total))
    update = jnp.sum(pull[:, None] * rows.astype(jnp.float32), axis=0).reshape(2, depth, shard)
    return (update[0], update[1].T, sample_weights)


def solution(mesh):
    in_specs = (P(("chain", "param"), None, None), P(), P(), P(), P(), P(), P(), P(), P(), P())
    out_specs = (P("chain", "param"), P("param", "chain"), P())
    run = functools.partial(body, mesh.shape["chain"], mesh.shape["param"])
    return jax.shard_map(run, mesh=mesh, in_specs=in_specs, out_specs=out_specs, check_vma=False)
```

```python
import functools
import math

import jax
import jax.numpy as jnp
from jax import lax
from jax.experimental import pallas as pl
from jax.experimental.pallas import tpu as pltpu
from jax.sharding import PartitionSpec as P

damping = 0.05
MESH = pl.DeviceIdType.MESH
slope = math.sqrt(2.0 / math.pi)
cubic = 0.044715


def dot(a, b, dims=((1,), (0,))):
    return lax.dot_general(a, b, (dims, ((), ())), preferred_element_type=jnp.float32)


def norm_columns(v):
    width = v.shape[0]
    centred = v - jnp.sum(v, axis=0, keepdims=True) * (1.0 / width)
    spread = jnp.sum(centred * centred, axis=0, keepdims=True) * (1.0 / width)
    return (centred * lax.rsqrt(spread + 1e-05)).astype(jnp.bfloat16)


def sum_kernel(n_chain, n_param, parts, out, landed, passed, total, sems):
    z, p = lax.axis_index("chain"), lax.axis_index("param")
    barrier = pltpu.get_barrier_semaphore()

    def in_plane(k):
        return (z, lax.rem(p + k, n_param))

    def in_chain(k):
        return (lax.rem(z + k, n_chain), p)

    def tell_plane(k, carry):
        pl.semaphore_signal(barrier, inc=1, device_id=in_plane(k), device_id_type=MESH)
        return carry

    def tell_chain(k, carry):
        pl.semaphore_signal(barrier, inc=1, device_id=in_chain(k), device_id_type=MESH)
        return carry

    lax.fori_loop(1, n_param, tell_plane, 0)
    lax.fori_loop(1, n_chain, tell_chain, 0)
    pl.semaphore_wait(barrier, n_chain + n_param - 2)

    def copy(source, target, phase, k, there):
        return pltpu.make_async_remote_copy(
            src_ref=source,
            dst_ref=target,
            send_sem=sems.at[phase, 0, k],
            recv_sem=sems.at[phase, 1, k],
            device_id=there,
            device_id_type=MESH,
        )

    def scatter(k):
        return copy(parts.at[lax.rem(p + k, n_param)], landed.at[p], 0, k, in_plane(k))

    def exchange(k):
        return copy(total.at[0], passed.at[z], 1, k, in_chain(k))

    def spread(k):
        return copy(total.at[1], out.at[p], 2, k, in_plane(k))

    def run(count, make, verb):
        def step(k, carry):
            getattr(make(k), verb)()
            return carry

        lax.fori_loop(1, count, step, 0)

    run(n_param, scatter, "start")
    landed[p] = parts[p]
    run(n_param, scatter, "wait")
    total[0] = jnp.sum(landed[...], axis=0)
    run(n_chain, exchange, "start")
    passed[z] = total[0]
    run(n_chain, exchange, "wait")
    total[1] = jnp.sum(passed[...], axis=0)
    run(n_param, spread, "start")
    out[p] = total[1]
    run(n_param, spread, "wait")


def forward_kernel(
    n_chain,
    n_param,
    mine,
    embed,
    position,
    value,
    mixing,
    out,
    up,
    down,
    readout,
    jac,
    position_t,
    value_t,
    out_t,
    up_t,
    down_t,
    readout_t,
    spins,
    stage,
    wide,
    spin_sems,
    send_sem,
    recv_sem,
):
    z, p = lax.axis_index("chain"), lax.axis_index("param")
    group, heads = embed.shape[0], mixing.shape[0]
    width, hidden_units = down_t.shape
    head_rows, depth, shard = width // heads, width // n_chain, hidden_units // n_param
    chunk = min(256, hidden_units)
    chunks = hidden_units // chunk

    barrier = pltpu.get_barrier_semaphore()

    def tell_chain(k, carry):
        there = (lax.rem(z + n_chain - k, n_chain), p)
        pl.semaphore_signal(barrier, inc=1, device_id=there, device_id_type=MESH)
        return carry

    def tell_plane(m, carry):
        there = (z, lax.rem(p + m, n_param))
        pl.semaphore_signal(barrier, inc=1, device_id=there, device_id_type=MESH)
        return carry

    lax.fori_loop(1, n_chain, tell_chain, 0)
    lax.fori_loop(1, n_param, tell_plane, 0)
    pl.semaphore_wait(barrier, n_chain + n_param - 2)

    def spin_copy(k):
        return pltpu.make_async_remote_copy(
            src_ref=mine,
            dst_ref=spins.at[z],
            send_sem=spin_sems.at[0, k],
            recv_sem=spin_sems.at[1, k],
            device_id=(lax.rem(z + n_chain - k, n_chain), p),
            device_id_type=MESH,
        )

    def slice_copy(g, k, m):
        owner = lax.rem(p + m, n_param)
        return pltpu.make_async_remote_copy(
            src_ref=stage.at[g, k, owner],
            dst_ref=jac.at[p, g, k],
            send_sem=send_sem.at[g, k, m],
            recv_sem=recv_sem.at[g, k, m],
            device_id=(z, owner),
            device_id_type=MESH,
        )

    def start_spins(k, carry):
        spin_copy(k).start()
        return carry

    lax.fori_loop(1, n_chain, start_spins, 0)
    spins[z] = mine[...]
    position_t[...] = position[...].astype(jnp.float32).T
    value_t[...] = value[...].T
    out_t[...] = out[...].T
    up_t[...] = up[...].T
    down_t[...] = down[...].T
    readout_t[...] = jnp.broadcast_to(readout[...], readout_t.shape[::-1]).T
    slab = pl.ds(pl.multiple_of(z * depth, depth), depth)

    def one_group(step, carry):
        @pl.when(step > 0)
        def _():
            spin_copy(step).wait_recv()

        g = lax.rem(z + step, n_chain)
        base = position_t[...]
        triple = jnp.concatenate([spins[g]] * 3, axis=0)
        embedded = [dot(embed[k], triple, ((0,), (0,))) + base for k in range(group)]
        values = [dot(value_t[...], norm_columns(e)).astype(jnp.bfloat16) for e in embedded]
        mixed = []
        for h in range(heads):
            rows = slice(h * head_rows, (h + 1) * head_rows)
            stacked = jnp.concatenate([v[rows] for v in values], axis=0)
            mixed.append(dot(stacked, mixing[h], ((1,), (1,))).astype(jnp.bfloat16))
        for k in range(group):
            rows = slice(k * head_rows, (k + 1) * head_rows)
            mixture = jnp.concatenate([m[rows] for m in mixed], axis=0)
            residual = embedded[k] + dot(out_t[...], mixture)
            features = norm_columns(residual)
            output = residual
            units, rises = [], []
            for c in range(chunks):
                rows = slice(c * chunk, (c + 1) * chunk)
                preact = dot(up_t[rows], features)
                squared = preact * preact
                bend = jnp.tanh(preact * (slope + (slope * cubic) * squared))
                half = 0.5 + 0.5 * bend
                hidden = (preact * half).astype(jnp.bfloat16)
                units.append(hidden)
                rises.append(
                    half
                    + (0.5 * preact)
                    * (1.0 - bend * bend)
                    * (slope + (3.0 * slope * cubic) * squared)
                )
                output = output + dot(down_t[:, rows], hidden)
            cotangent = (readout_t[...] * jnp.tanh(output)).astype(jnp.bfloat16)
            wide[k % 2, 0] = features
            wide[k % 2, 1] = cotangent
            left, right = wide[k % 2, 0, slab, :], wide[k % 2, 1, slab, :]
            for c in range(chunks):
                rows = slice(c * chunk, (c + 1) * chunk)
                grad = (rises[c] * dot(down[rows], cotangent)).astype(jnp.bfloat16)
                up_block = dot(left, grad, ((1,), (1,))).astype(jnp.bfloat16)
                down_block = dot(right, units[c], ((1,), (1,))).astype(jnp.bfloat16)
                for part in range(chunk // shard):
                    columns = slice(part * shard, (part + 1) * shard)
                    owner = c * (chunk // shard) + part
                    stage[g, k, owner, :depth, :] = up_block[:, columns]
                    stage[g, k, owner, depth:, :] = down_block[:, columns]

            def start_slices(m, carry):
                slice_copy(g, k, m).start()
                return carry

            lax.fori_loop(1, n_param, start_slices, 0)
            jac[p, g, k] = stage[g, k, p]
        return carry

    lax.fori_loop(0, n_chain, one_group, 0)

    def end_spins(k, carry):
        spin_copy(k).wait_send()
        return carry

    lax.fori_loop(1, n_chain, end_spins, 0)

    def end_slices(i, carry):
        m = 1 + lax.rem(i, n_param - 1)
        gk = i // (n_param - 1)
        slice_copy(gk // group, lax.rem(gk, group), m).wait()
        return carry

    lax.fori_loop(0, n_chain * group * (n_param - 1), end_slices, 0)


def solve_kernel(raw, energy, solved):
    size = raw.shape[0]
    tile = 8
    gram = raw[...]
    by_row = jnp.mean(gram, axis=0, keepdims=True)
    by_column = jnp.mean(gram, axis=1, keepdims=True)
    gram = (gram - by_row - by_column + jnp.mean(by_row, axis=1, keepdims=True)) * (1.0 / size)
    row = lax.broadcasted_iota(jnp.int32, (size, size), 0)
    column = lax.broadcasted_iota(jnp.int32, (size, size), 1)
    same = row == column
    diagonal = jnp.sum(jnp.where(same, gram, 0.0), axis=0, keepdims=True)
    scale = jnp.sum(diagonal, axis=1, keepdims=True) * (1.0 / size)
    system = gram + jnp.where(same, damping * scale, 0.0)
    right = jnp.broadcast_to(energy[...], (size, size)).T
    rest = jnp.concatenate([system, right], axis=1)
    sub = lax.broadcasted_iota(jnp.int32, (tile, size), 0)
    lane = lax.broadcasted_iota(jnp.int32, (tile, size), 1)

    def across(block, i):
        return jnp.broadcast_to(block[i : i + 1], block.shape)

    saved = []
    for start in range(0, size, tile):
        left, aim = rest[:tile, :size], rest[:tile, size:]
        columns = [
            jnp.broadcast_to(left[:, start + j : start + j + 1], (tile, size)) for j in range(tile)
        ]
        inverse = jnp.zeros((tile, size), jnp.float32)
        for i in range(tile):
            over = 1.0 / across(columns[i], i)
            inverse = jnp.where(sub == i, over, inverse)
            factor = jnp.where(sub > i, columns[i] * over, 0.0)
            left = left - factor * across(left, i)
            aim = aim - factor * across(aim, i)
            for j in range(i + 1, tile):
                columns[j] = columns[j] - factor * across(columns[j], i)
        saved.append((left, aim, columns, inverse))
        if start + tile < size:
            scaled = jnp.concatenate([left * inverse, aim * inverse], axis=1)
            taken = lax.dot_general(
                left,
                scaled,
                (((0,), (0,)), ((), ())),
                precision=lax.Precision.HIGHEST,
                preferred_element_type=jnp.float32,
            )
            rest = rest[tile:] - taken[start + tile :]
    answer = jnp.zeros((tile, size), jnp.float32)
    for start in range(size - tile, -1, -tile):
        left, aim, columns, inverse = saved[start // tile]
        aim = aim - jnp.sum(left * answer, axis=1, keepdims=True)
        for i in range(tile - 1, -1, -1):
            found = across(aim * inverse, i)
            answer = jnp.where(lane == start + i, found, answer)
            aim = aim - columns[i] * found
    solved[...] = answer[:1] * scale


def solve_weights(gram, energy, total):
    scale = jnp.trace(gram) / total
    system = gram + damping * scale * jnp.eye(total, dtype=jnp.float32)
    lower = jnp.linalg.cholesky(system)
    column = energy[:, None]
    middle = lax.linalg.triangular_solve(lower, column, left_side=True, lower=True)
    answer = lax.linalg.triangular_solve(
        lower, middle, left_side=True, lower=True, transpose_a=True
    )
    return scale * answer[:, 0]


def body(
    n_chain,
    n_param,
    spins,
    local_energy,
    embed_weight,
    position,
    value_weight,
    mixing,
    out_weight,
    up_weight,
    down_weight,
    readout,
):
    samples, patches, sites = spins.shape
    total = local_energy.shape[0]
    width, hidden_units = up_weight.shape
    heads = mixing.shape[0]
    depth, shard = width // n_chain, hidden_units // n_param
    vmem = pl.BlockSpec(memory_space=pltpu.VMEM)

    signs = (2 * spins - 1).astype(jnp.bfloat16)
    signs = signs.transpose(0, 2, 1).reshape(samples * sites, patches)
    high = lax.reduce_precision(embed_weight, 8, 7)
    middle = lax.reduce_precision(embed_weight - high, 8, 7)
    low = embed_weight - high - middle
    parts = jnp.stack([high, middle, low]).astype(jnp.bfloat16)
    pick = jnp.eye(samples, dtype=jnp.bfloat16)
    embed = pick[:, None, :, None, None] * parts[:, None, :, :]
    embed = embed.reshape(samples, 3 * samples * sites, width)

    sems = (n_chain, samples, n_param)
    jac = pl.pallas_call(
        functools.partial(forward_kernel, n_chain, n_param),
        out_shape=jax.ShapeDtypeStruct(
            (n_param, n_chain, samples, 2 * depth, shard), jnp.bfloat16
        ),
        in_specs=[vmem] * 9,
        out_specs=vmem,
        scratch_shapes=[
            pltpu.VMEM((width, patches), jnp.float32),
            pltpu.VMEM((width, width), jnp.bfloat16),
            pltpu.VMEM((width, width), jnp.bfloat16),
            pltpu.VMEM((hidden_units, width), jnp.bfloat16),
            pltpu.VMEM((width, hidden_units), jnp.bfloat16),
            pltpu.VMEM((width, patches), jnp.float32),
            pltpu.VMEM((n_chain, samples * sites, patches), jnp.bfloat16),
            pltpu.VMEM((n_chain, samples, n_param, 2 * depth, shard), jnp.bfloat16),
            pltpu.VMEM((2, 2, width, patches), jnp.bfloat16),
            pltpu.SemaphoreType.DMA((2, n_chain)),
            pltpu.SemaphoreType.DMA(sems),
            pltpu.SemaphoreType.DMA(sems),
        ],
        compiler_params=pltpu.CompilerParams(
            collective_id=0, has_side_effects=True, vmem_limit_bytes=56 * 2**20
        ),
    )(
        signs,
        embed,
        position,
        value_weight,
        mixing,
        out_weight,
        up_weight,
        down_weight,
        readout[None, :],
    )
    rows = lax.optimization_barrier(jac.reshape(total, 2 * depth * shard))
    raw = lax.dot_general(
        rows, rows, (((1,), (1,)), ((), ())), preferred_element_type=jnp.float32
    )
    share = total // n_param
    raw = pl.pallas_call(
        functools.partial(sum_kernel, n_chain, n_param),
        out_shape=jax.ShapeDtypeStruct((n_param, share, total), jnp.float32),
        in_specs=[vmem],
        out_specs=vmem,
        scratch_shapes=[
            pltpu.VMEM((n_param, share, total), jnp.float32),
            pltpu.VMEM((n_chain, share, total), jnp.float32),
            pltpu.VMEM((2, share, total), jnp.float32),
            pltpu.SemaphoreType.DMA((3, 2, max(n_chain, n_param))),
        ],
        compiler_params=pltpu.CompilerParams(
            collective_id=1, has_side_effects=True, vmem_limit_bytes=32 * 2**20
        ),
    )(raw.reshape(n_param, share, total)).reshape(total, total)
    energy = (local_energy - jnp.mean(local_energy)) / math.sqrt(total)
    energy = energy.reshape(n_chain, n_param, samples).swapaxes(0, 1).reshape(total)
    if total <= 128 and total % 8 == 0:
        solved = pl.pallas_call(
            solve_kernel,
            out_shape=jax.ShapeDtypeStruct((1, total), jnp.float32),
            in_specs=[vmem, vmem],
            out_specs=vmem,
            compiler_params=pltpu.CompilerParams(vmem_limit_bytes=24 * 2**20),
        )(raw, energy[None, :])[0]
    else:
        average = jnp.mean(raw, axis=0)
        gram = (raw - average[None, :] - average[:, None] + jnp.mean(average)) / total
        solved = solve_weights(gram, energy, total)
    sample_weights = solved.reshape(n_param, n_chain, samples).swapaxes(0, 1).reshape(total)
    pull = (solved - jnp.mean(solved)) * (-1.0 / math.sqrt(total))
    update = jnp.sum(pull[:, None] * rows.astype(jnp.float32), axis=0).reshape(2, depth, shard)
    return (update[0], update[1].T, sample_weights)


def solution(mesh):
    in_specs = (P(("chain", "param"), None, None), P(), P(), P(), P(), P(), P(), P(), P(), P())
    out_specs = (P("chain", "param"), P("param", "chain"), P())
    run = functools.partial(body, mesh.shape["chain"], mesh.shape["param"])
    return jax.shard_map(run, mesh=mesh, in_specs=in_specs, out_specs=out_specs, check_vma=False)
```
